32 devices in a mesh: dp: 8 (over z, x), tensor: 4 (over y, core).
Axes of the slice: x: 2, y: 2, z: 4, core: 2. Of those that a mesh axis runs over, the one named last changes fastest.
Arguments:
- query: bfloat16 [2048, 5120], P('dp', 'tensor'), may hold values from -140 to 140
- keys_values: bfloat16 [2, 2048, 1024], P(None, 'dp', 'tensor'), may hold values from -6 to 6
- out_weight: bfloat16 [5120, 5120], P(('tensor', 'dp')), may hold values from -0.5 to 0.5
- parents: int32 [8], replicated, may hold values from -1 to 6, as said below
- lengths: int32 [8], replicated, may hold values from 1 to 256, 1024 in all
Outputs:
- projected: bfloat16 [2048, 5120], P('dp', 'tensor')
The draws below stay inside these ranges and needn't reach their ends.
Inputs may be any that keep to these rules, and one draw needn't show every extreme that they name: parents[n] is -1 for a root, else a node before n; every ancestor of n lies among the 3 nodes before n; node 0 is a root; node 4 has the node before it as parent, that one the node before it, and that one the node before it, which is a root.
All inputs are finite; a program needn't handle non-finite values.
Results may differ from the reference program's by a relative error of at most 0.0053.
Values may be sent and summed in bfloat16 or wider, within the bound.
No kernel may reach another device: no remote copies, remote signals or barrier semaphores. Data moves between devices by JAX's collectives and lax.ppermute only.
A program may use at most 64 MiB of HBM per device.

```python
import math
import jax
import jax.numpy as jnp
import numpy as np
from jax import lax

D = 5120
HEADS = 40
KV_HEADS = 8
HEAD_DIM = 128
CAP = 256
ANC = 3
NODES = 8
TOKENS = 2048
LIVE_DEV = 128


def draw_parents(key, part):
    starts = jax.random.randint(jax.random.fold_in(key, 21), (NODES,), 0, 3)
    picks = jax.random.randint(jax.random.fold_in(key, 22), (NODES,), 0, 1 << 20)
    middle = NODES // 2

    def advance(group_start, inputs):
        node_index, start_draw, pick = inputs
        fresh = (start_draw == 0) & (node_index > ANC) | (node_index - group_start > ANC) | (node_index == 0)
        forced_root = (node_index == middle - ANC) | (node_index == middle + 1)
        forced_chain = (node_index > middle - ANC) & (node_index <= middle)
        fresh = (fresh | forced_root) & jnp.logical_not(forced_chain)
        span_size = jnp.maximum(node_index - group_start, 1)
        chosen = jnp.where(forced_chain, node_index - 1, node_index - 1 - pick % span_size)
        parent = jnp.where(fresh, -1, chosen)
        return (jnp.where(fresh, node_index, group_start), parent)
    final_start, parent_list = lax.scan(advance, jnp.int32(0), (jnp.arange(NODES, dtype=jnp.int32), starts, picks))
    return parent_list.astype(jnp.int32)


def draw_query(key, part):
    width = HEADS * HEAD_DIM
    return jnp.clip(jax.random.normal(jax.random.fold_in(key, 35), (TOKENS, width), jnp.float32), -6.0, 6.0).astype(jnp.bfloat16)


def draw_keys_values(key, part):
    width = KV_HEADS * HEAD_DIM
    return jnp.clip(jax.random.normal(jax.random.fold_in(key, 45), (2, TOKENS, width), jnp.float32), -6.0, 6.0).astype(jnp.bfloat16)


def block_levels(key, shape, cuts, least, high):
    def one(dim, shards_of):
        heights = jax.random.uniform(jax.random.fold_in(jax.random.fold_in(key, 6), dim), (shards_of,), jnp.float32, least / len(cuts), high / len(cuts))
        return jnp.repeat(jnp.exp(heights), shape[dim] // shards_of).reshape((-1,) + (1,) * (len(shape) - dim - 1))

    gain = one(*cuts[0])
    for cut in cuts[1:]:
        gain = gain * one(*cut)
    return gain


def profile(amount, total, most, lean):
    portions = [(1 << 20) // math.isqrt(rank ** lean) + 1 for rank in range(2, amount + 1)]
    rest, counts = total - most - (amount - 1), [1] * (amount - 1)
    while rest > 0:
        free = [i for i in range(amount - 1) if counts[i] < most]
        mass, remaining = sum([portions[i] for i in free]), rest
        for i in free:
            addition = min(most - counts[i], max(1, remaining * portions[i] // mass), rest)
            counts[i] = counts[i] + addition
            rest = rest - addition
    return np.array([most] + counts)


def uneven(key, count, total, bound, slope):
    if count == 2:
        one = jax.random.randint(key, (), max(1, total - bound), min(bound, total - 1) + 1)
        return jnp.stack([one, total - one])
    sizes = jnp.asarray(profile(count, total, bound, slope), jnp.int32)
    pairs = (count - 1) // 2
    giver, receiver = sizes[1:1 + 2 * pairs:2], sizes[2:2 + 2 * pairs:2]
    margin = jnp.minimum(giver - 1, bound - receiver)
    shifted = jax.random.randint(jax.random.fold_in(key, 1), (pairs,), 0, 1 << 20) % (margin + 1)
    sizes = sizes.at[1:1 + 2 * pairs:2].set(giver - shifted).at[2:2 + 2 * pairs:2].set(receiver + shifted)
    return sizes[jax.random.permutation(jax.random.fold_in(key, 2), count)]


def scatter_about(own_key, dims, scale, most, cuts=(), kind=jnp.bfloat16):
    array = jax.random.normal(own_key, dims, jnp.float32) * scale
    if len(cuts) > 0:
        array = block_levels(own_key, dims, cuts, -0.22, 0.18) * array
    return jnp.clip(array, min=-most, max=most).astype(kind)


def setup_inputs(seed: int = 0) -> dict:
    streams_of = jax.random.split(jax.random.key(seed), 6)
    query = draw_query(jax.random.fold_in(streams_of[5], 71), 0)
    keys_values = draw_keys_values(jax.random.fold_in(streams_of[5], 71), 0)
    out_weight = scatter_about(streams_of[2], (HEADS * HEAD_DIM, D), HEAD_DIM ** -0.5, 0.5, ((0, 32),))
    parents = draw_parents(jax.random.fold_in(streams_of[5], 71), 0)
    lengths = uneven(streams_of[4], NODES, NODES * LIVE_DEV, CAP, 2).astype(jnp.int32)
    return {"query": query, "keys_values": keys_values, "out_weight": out_weight, "parents": parents, "lengths": lengths}


neg_big = -1.0e30


def reference(query, keys_values, out_weight, parents, lengths):
    nodes = parents.shape[0]
    capacity = query.shape[0] // nodes
    per_group = HEADS // KV_HEADS
    score_scale = HEAD_DIM ** -0.5
    positions = jnp.arange(capacity, dtype=jnp.int32)
    node_ids = jnp.arange(nodes, dtype=jnp.int32)
    spans = jnp.arange(ANC + 1, dtype=jnp.int32)
    ancestry = jnp.zeros((nodes, ANC + 1), jnp.int32)
    climber = parents
    for climb_step in range(ANC):
        hit = (climber >= 0)[:, None] & (spans[None, :] == (node_ids - climber)[:, None])
        ancestry = jnp.where(hit, 1, ancestry)
        climber = jnp.where(climber >= 0, parents[jnp.maximum(climber, 0)], -1)
    queries = query.reshape(nodes, capacity, KV_HEADS, per_group, HEAD_DIM)
    pairs = keys_values.reshape(2, nodes, capacity, KV_HEADS, HEAD_DIM)

    def one_node(node_index):
        own_queries = queries[node_index].astype(jnp.float32)
        key_list = []
        value_list = []
        mask_list = []
        for distance in range(ANC + 1):
            source = jnp.maximum(node_index - distance, 0).astype(jnp.int32)
            key_list.append(pairs[0, source])
            value_list.append(pairs[1, source])
            within = positions[None, :] < lengths[source]
            if distance == 0:
                allowed = within & (positions[None, :] <= positions[:, None])
            else:
                allowed = within & (ancestry[node_index, distance] > 0) & (node_index - distance >= 0)
                allowed = jnp.broadcast_to(allowed, (capacity, capacity))
            mask_list.append(allowed)
        key_all = jnp.concatenate(key_list, 0).astype(jnp.float32)
        value_all = jnp.concatenate(value_list, 0).astype(jnp.float32)
        mask_all = jnp.concatenate(mask_list, 1)
        scores = jnp.einsum("irhd,jrd->rhij", own_queries, key_all) * score_scale
        scores = jnp.where(mask_all[None, None], scores, neg_big)
        row_max = jnp.max(scores, axis=-1, keepdims=True)
        weights = jnp.where(mask_all[None, None], jnp.exp(scores - row_max), 0.0)
        row_sum = jnp.sum(weights, axis=-1, keepdims=True)
        rounded = lax.optimization_barrier(weights.astype(jnp.bfloat16)).astype(jnp.float32)
        mixed = jnp.einsum("rhij,jrd->rhid", rounded, value_all) / row_sum
        mixed = jnp.transpose(mixed, (2, 0, 1, 3))
        mixed = jnp.where(positions[:, None, None, None] < lengths[node_index], mixed, 0.0)
        return mixed.reshape(capacity, HEADS * HEAD_DIM).astype(jnp.bfloat16)

    attended = lax.map(one_node, node_ids).reshape(nodes * capacity, HEADS * HEAD_DIM)
    return jnp.dot(attended, out_weight, preferred_element_type=jnp.float32).astype(jnp.bfloat16)
```

```python
import functools

import jax
import jax.numpy as jnp
from jax import lax
from jax.sharding import Mesh
from jax.sharding import PartitionSpec as P

HEAD_DIM = 128
ANC = 3
NEG_BIG = -1e30

NODE_AXES = ("h", "q", "l", "x")
HEAD_AXES = ("y", "c")


def swapped(value, axis):
    return lax.ppermute(value, axis, [(0, 1), (1, 0)])


def passed_along(value, by):
    size = lax.axis_size(NODE_AXES)
    pairs = [(i, i + by) for i in range(size - by)]
    return lax.ppermute(value, NODE_AXES, pairs)


def attention_limits(node, parents, lengths):
    spans = jnp.arange(ANC + 1, dtype=jnp.int32)
    sources = jnp.maximum(node - spans, 0)
    seen = spans == 0
    climber = parents[node]
    for _ in range(ANC):
        seen = seen | ((climber >= 0) & (spans == node - climber))
        climber = jnp.where(climber >= 0, parents[jnp.maximum(climber, 0)], -1)
    return jnp.where(seen, lengths[sources], 0)


def attend(half, limits, query, kv_blocks):
    capacity, width = query.shape[0], query.shape[1] // 2
    kv_width = kv_blocks[0].shape[2] // 2
    kv_count = kv_width // HEAD_DIM
    per_group = width // kv_width
    score_scale = HEAD_DIM ** (-0.5)
    positions = jnp.arange(capacity, dtype=jnp.int32)
    queries = columns_of(query, half, 2).reshape(capacity, kv_count, per_group, HEAD_DIM)
    pairs = [
        lax.dynamic_slice_in_dim(kv, half * kv_width, kv_width, 2).reshape(2, capacity, kv_count, HEAD_DIM)
        for kv in kv_blocks
    ]
    scores = []
    for distance, pair in enumerate(pairs):
        allowed = jnp.broadcast_to(positions[None, :] < limits[distance], (capacity, capacity))
        if distance == 0:
            allowed = allowed & (positions[None, :] <= positions[:, None])
        s = jnp.einsum("irgd,jrd->rgij", queries, pair[0], preferred_element_type=jnp.float32)
        scores.append(jnp.where(allowed, s * score_scale, NEG_BIG))
    row_max = functools.reduce(jnp.maximum, [s.max(axis=-1, keepdims=True) for s in scores])
    weights = [jnp.exp(s - row_max) for s in scores]
    row_sum = sum(w.sum(axis=-1, keepdims=True) for w in weights)
    total = sum(
        jnp.einsum("rgij,jrd->rgid", w.astype(jnp.bfloat16), pair[1], preferred_element_type=jnp.float32)
        for w, pair in zip(weights, pairs)
    )
    mixed = jnp.transpose(total / row_sum, (2, 0, 1, 3)).reshape(capacity, width)
    return jnp.where(positions[:, None] < limits[0], mixed, 0.0).astype(jnp.bfloat16)


def columns_of(value, index, parts):
    width = value.shape[1] // parts
    return lax.dynamic_slice_in_dim(value, index * width, width, 1)


def per_device(query, keys_values, out_weight, parents, lengths):
    h, l, x = lax.axis_index("h"), lax.axis_index("l"), lax.axis_index("x")
    y, c = lax.axis_index("y"), lax.axis_index("c")
    node = lax.axis_index(NODE_AXES)
    limits = attention_limits(node, parents, lengths)
    kv_blocks = [keys_values] + [passed_along(keys_values, d) for d in range(1, ANC + 1)]

    parts = lax.axis_size("q")
    if parts > 1:
        out_weight = lax.all_gather(out_weight, "q", axis=0, tiled=True)
    own = columns_of(out_weight, y, 2)
    own_y = swapped(columns_of(out_weight, 1 - y, 2), "y")
    own_x, own_l = swapped(own, "x"), swapped(own, "l")
    y_x, y_l = swapped(own_y, "x"), swapped(own_y, "l")
    own_lx, y_lx = swapped(own_l, "x"), swapped(y_x, "l")
    pieces = [own, own_x, own_l, own_lx, own_y, y_x, y_l, y_lx]

    sent = attend(1 - h, limits, query, kv_blocks)
    far = swapped(sent, "h")
    near = attend(h, limits, query, kv_blocks)

    def blocks_of(attended):
        tokens = attended.shape[0]
        b = attended.reshape(tokens, parts, 2, 2, -1)
        b = jnp.where(x > 0, b[:, :, :, ::-1], b)
        b = jnp.where(l > 0, b[:, :, ::-1], b)
        return [b[:, :, i, j].reshape(tokens, -1) for i in range(2) for j in range(2)]

    def summed(attended):
        blocks = blocks_of(attended) + blocks_of(swapped(attended, "y"))
        total = sum(jnp.dot(a, w, preferred_element_type=jnp.float32) for a, w in zip(blocks, pieces))
        return columns_of(total, c, 2) + swapped(columns_of(total, 1 - c, 2), "c")

    arrived = swapped(summed(far).astype(jnp.bfloat16), "h")
    return (summed(near) + arrived.astype(jnp.float32)).astype(jnp.bfloat16)


def solution(mesh):
    dp, tensor = mesh.shape["dp"], mesh.shape["tensor"]
    fine = Mesh(mesh.devices.reshape(2, dp // 8, 2, 2, 2, tensor // 2), NODE_AXES + HEAD_AXES)
    return jax.shard_map(
        per_device,
        mesh=fine,
        in_specs=(
            P(NODE_AXES, HEAD_AXES),
            P(None, NODE_AXES, HEAD_AXES),
            P(HEAD_AXES + NODE_AXES, None),
            P(),
            P(),
        ),
        out_specs=P(NODE_AXES, HEAD_AXES),
        check_vma=False,
    )
```

```python
import functools

import jax
import jax.numpy as jnp
from jax import lax
from jax.sharding import Mesh
from jax.sharding import PartitionSpec as P

HEAD_DIM = 128
ANC = 3
NEG_BIG = -1e30
CHUNKS = 2

NODE_AXES = ("h", "q", "l", "x")
HEAD_AXES = ("y", "c")


def swapped(value, axis):
    return lax.ppermute(value, axis, [(0, 1), (1, 0)])


def passed_along(value, by):
    size = lax.axis_size(NODE_AXES)
    return lax.ppermute(value, NODE_AXES, [(i, (i + by) % size) for i in range(size)])


def attention_limits(node, parents, lengths):
    spans = jnp.arange(ANC + 1, dtype=jnp.int32)
    sources = jnp.maximum(node - spans, 0)
    seen = spans == 0
    climber = parents[node]
    for _ in range(ANC):
        seen = seen | ((climber >= 0) & (spans == node - climber))
        climber = jnp.where(climber >= 0, parents[jnp.maximum(climber, 0)], -1)
    return jnp.where(seen, lengths[sources], 0)


def attend(half, limits, query, kv_blocks):
    capacity, width = query.shape[0], query.shape[1] // 2
    kv_width = kv_blocks[0].shape[2] // 2
    kv_count = kv_width // HEAD_DIM
    per_group = width // kv_width
    score_scale = HEAD_DIM ** (-0.5)
    positions = jnp.arange(capacity, dtype=jnp.int32)
    queries = columns_of(query, half, 2).reshape(capacity, kv_count, per_group, HEAD_DIM)
    pairs = [
        lax.dynamic_slice_in_dim(kv, half * kv_width, kv_width, 2).reshape(2, capacity, kv_count, HEAD_DIM)
        for kv in kv_blocks
    ]
    scores = []
    for distance, pair in enumerate(pairs):
        allowed = jnp.broadcast_to(positions[None, :] < limits[distance], (capacity, capacity))
        if distance == 0:
            allowed = allowed & (positions[None, :] <= positions[:, None])
        s = jnp.einsum("irgd,jrd->rgij", queries, pair[0], preferred_element_type=jnp.float32)
        scores.append(jnp.where(allowed, s * score_scale, NEG_BIG))
    row_max = functools.reduce(jnp.maximum, [s.max(axis=-1, keepdims=True) for s in scores])
    weights = [jnp.exp(s - row_max) for s in scores]
    row_sum = sum(w.sum(axis=-1, keepdims=True) for w in weights)
    total = sum(
        jnp.einsum("rgij,jrd->rgid", w.astype(jnp.bfloat16), pair[1], preferred_element_type=jnp.float32)
        for w, pair in zip(weights, pairs)
    )
    mixed = jnp.transpose(total / row_sum, (2, 0, 1, 3)).reshape(capacity, width)
    return jnp.where(positions[:, None] < limits[0], mixed, 0.0).astype(jnp.bfloat16)


def columns_of(value, index, parts):
    width = value.shape[1] // parts
    return lax.dynamic_slice_in_dim(value, index * width, width, 1)


def per_device(query, keys_values, out_weight, parents, lengths):
    h, l, x = lax.axis_index("h"), lax.axis_index("l"), lax.axis_index("x")
    y, c = lax.axis_index("y"), lax.axis_index("c")
    node = lax.axis_index(NODE_AXES)
    limits = attention_limits(node, parents, lengths)
    kv_blocks = [keys_values] + [passed_along(keys_values, d) for d in range(1, ANC + 1)]

    parts = lax.axis_size("q")
    if parts > 1:
        out_weight = lax.all_gather(out_weight, "q", axis=0, tiled=True)
    width = out_weight.shape[1] // 4
    step = width // CHUNKS

    def chunk_of(y_index, chunk):
        starts = [(y_index * 2 + c_index) * width + chunk * step for c_index in (1 - c, c)]
        return jnp.concatenate([lax.dynamic_slice_in_dim(out_weight, s, step, 1) for s in starts], 1)

    chunks = []
    for chunk in range(CHUNKS):
        own_y = swapped(chunk_of(1 - y, chunk), "y")
        own = chunk_of(y, chunk)
        own_x, own_l = swapped(own, "x"), swapped(own, "l")
        y_x, y_l = swapped(own_y, "x"), swapped(own_y, "l")
        own_lx, y_lx = swapped(own_l, "x"), swapped(y_x, "l")
        chunks.append([own, own_x, own_l, own_lx, own_y, y_x, y_l, y_lx])

    sent = attend(1 - h, limits, query, kv_blocks)
    far = swapped(sent, "h")
    near = attend(h, limits, query, kv_blocks)

    def blocks_of(attended):
        tokens = attended.shape[0]
        b = attended.reshape(tokens, parts, 2, 2, -1)
        b = jnp.where(x > 0, b[:, :, :, ::-1], b)
        b = jnp.where(l > 0, b[:, :, ::-1], b)
        return [b[:, :, i, j].reshape(tokens, -1) for i in range(2) for j in range(2)]

    near_blocks = blocks_of(near) + blocks_of(swapped(near, "y"))
    far_blocks = blocks_of(far) + blocks_of(swapped(far, "y"))

    def summed(blocks, pieces):
        total = sum(jnp.dot(a, w, preferred_element_type=jnp.float32) for a, w in zip(blocks, pieces))
        return total[:, step:] + swapped(total[:, :step], "c")

    outputs = []
    for pieces in chunks:
        arrived = swapped(summed(far_blocks, pieces).astype(jnp.bfloat16), "h")
        outputs.append((summed(near_blocks, pieces) + arrived.astype(jnp.float32)).astype(jnp.bfloat16))
    return jnp.concatenate(outputs, 1)


def solution(mesh):
    dp, tensor = mesh.shape["dp"], mesh.shape["tensor"]
    fine = Mesh(mesh.devices.reshape(2, dp // 8, 2, 2, 2, tensor // 2), NODE_AXES + HEAD_AXES)
    return jax.shard_map(
        per_device,
        mesh=fine,
        in_specs=(
            P(NODE_AXES, HEAD_AXES),
            P(None, NODE_AXES, HEAD_AXES),
            P(HEAD_AXES + NODE_AXES, None),
            P(),
            P(),
        ),
        out_specs=P(NODE_AXES, HEAD_AXES),
        check_vma=False,
    )
```

```python
import functools

import jax
import jax.numpy as jnp
from jax import lax
from jax.experimental import pallas as pl
from jax.experimental.pallas import tpu as pltpu
from jax.sharding import Mesh
from jax.sharding import PartitionSpec as P

HEAD_DIM = 128
ANC = 3
NEG_BIG = -1e30
CHUNKS = 1

NODE_AXES = ("h", "q", "l", "x")
HEAD_AXES = ("y", "c")


def swapped(value, axis):
    return lax.ppermute(value, axis, [(0, 1), (1, 0)])


def passed_along(value, by):
    size = lax.axis_size(NODE_AXES)
    return lax.ppermute(value, NODE_AXES, [(i, (i + by) % size) for i in range(size)])


def attend_kernel(where_ref, parents_ref, lengths_ref, query_ref, *refs):
    kv_refs, out_ref = refs[: ANC + 1], refs[ANC + 1]
    node = where_ref[1]
    capacity = query_ref.shape[0]
    kv_count = kv_refs[0].shape[2] // HEAD_DIM
    per_group = query_ref.shape[1] // HEAD_DIM // kv_count
    score_scale = HEAD_DIM ** (-0.5)
    limits = [lengths_ref[node]] + [jnp.int32(0)] * ANC
    climber = parents_ref[node]
    for _ in range(ANC):
        reached = jnp.maximum(climber, 0)
        for distance in range(1, ANC + 1):
            hit = (climber >= 0) & (node - climber == distance)
            limits[distance] = jnp.where(hit, lengths_ref[reached], limits[distance])
        climber = jnp.where(climber >= 0, parents_ref[reached], -1)
    row = lax.broadcasted_iota(jnp.int32, (capacity, capacity), 0)
    col = lax.broadcasted_iota(jnp.int32, (capacity, capacity), 1)
    masks = [(col <= row) & (col < limits[0])] + [col < limits[d] for d in range(1, ANC + 1)]
    live = lax.broadcasted_iota(jnp.int32, (capacity, HEAD_DIM), 0) < limits[0]
    for kv_head in range(kv_count):
        kv_cols = slice(kv_head * HEAD_DIM, (kv_head + 1) * HEAD_DIM)
        for member in range(per_group):
            head = kv_head * per_group + member
            cols = slice(head * HEAD_DIM, (head + 1) * HEAD_DIM)
            q = query_ref[:, cols]
            scores = []
            for kv_ref, mask in zip(kv_refs, masks):
                s = lax.dot_general(
                    q, kv_ref[0, :, kv_cols], (((1,), (1,)), ((), ())), preferred_element_type=jnp.float32
                )
                scores.append(jnp.where(mask, s * score_scale, NEG_BIG))
            row_max = functools.reduce(jnp.maximum, scores).max(axis=1, keepdims=True)
            weights = [jnp.exp(s - row_max) for s in scores]
            row_sum = functools.reduce(jnp.add, weights).sum(axis=1, keepdims=True)
            total = jnp.zeros((capacity, HEAD_DIM), jnp.float32)
            for kv_ref, w in zip(kv_refs, weights):
                total = total + jnp.dot(
                    w.astype(jnp.bfloat16), kv_ref[1, :, kv_cols], preferred_element_type=jnp.float32
                )
            out_ref[:, cols] = jnp.where(live, total / row_sum, 0.0).astype(out_ref.dtype)


def attend(half, node, parents, lengths, query, kv_blocks):
    capacity, width = query.shape[0], query.shape[1] // 2
    kv_width = kv_blocks[0].shape[2] // 2
    return pl.pallas_call(
        attend_kernel,
        out_shape=jax.ShapeDtypeStruct((capacity, width), jnp.bfloat16),
        grid_spec=pltpu.PrefetchScalarGridSpec(
            num_scalar_prefetch=3,
            grid=(1,),
            in_specs=[pl.BlockSpec((capacity, width), lambda i, w, p, n: (0, w[0]))]
            + [pl.BlockSpec((2, capacity, kv_width), lambda i, w, p, n: (0, 0, w[0]))] * (ANC + 1),
            out_specs=pl.BlockSpec((capacity, width), lambda i, w, p, n: (0, 0)),
        ),
        compiler_params=pltpu.CompilerParams(vmem_limit_bytes=8 * 2**20),
        cost_estimate=pl.CostEstimate(
            flops=capacity * capacity * (ANC + 1) * width,
            bytes_accessed=4 * capacity * width + 4 * capacity * kv_width * (ANC + 1),
            transcendentals=capacity * capacity * (ANC + 1) * width // HEAD_DIM,
        ),
    )(jnp.stack([half, node]).astype(jnp.int32), parents, lengths, query, *kv_blocks)


def per_device(query, keys_values, out_weight, parents, lengths):
    h, l, x = lax.axis_index("h"), lax.axis_index("l"), lax.axis_index("x")
    y, c = lax.axis_index("y"), lax.axis_index("c")
    node = lax.axis_index(NODE_AXES)
    kv_blocks = [keys_values] + [passed_along(keys_values, d) for d in range(1, ANC + 1)]

    parts = lax.axis_size("q")
    if parts > 1:
        out_weight = lax.all_gather(out_weight, "q", axis=0, tiled=True)
    width = out_weight.shape[1] // 4
    step = width // CHUNKS

    def chunk_of(y_index, chunk):
        starts = [(y_index * 2 + c_index) * width + chunk * step for c_index in (1 - c, c)]
        return jnp.concatenate([lax.dynamic_slice_in_dim(out_weight, s, step, 1) for s in starts], 1)

    chunks = []
    for chunk in range(CHUNKS):
        own_y = swapped(chunk_of(1 - y, chunk), "y")
        own = chunk_of(y, chunk)
        own_x, own_l = swapped(own, "x"), swapped(own, "l")
        y_x, y_l = swapped(own_y, "x"), swapped(own_y, "l")
        own_lx, y_lx = swapped(own_l, "x"), swapped(y_x, "l")
        chunks.append([own, own_x, own_l, own_lx, own_y, y_x, y_l, y_lx])

    sent = attend(1 - h, node, parents, lengths, query, kv_blocks)
    far = swapped(sent, "h")
    near = attend(h, node, parents, lengths, query, kv_blocks)

    def blocks_of(attended):
        tokens = attended.shape[0]
        split = attended.reshape(tokens, parts, 4, -1)
        b = [split[:, :, i].reshape(tokens, -1) for i in range(4)]
        b = [jnp.where(x > 0, b[i ^ 1], b[i]) for i in range(4)]
        return [jnp.where(l > 0, b[i ^ 2], b[i]) for i in range(4)]

    near_blocks = blocks_of(near) + blocks_of(swapped(near, "y"))
    far_blocks = blocks_of(far) + blocks_of(swapped(far, "y"))

    def summed(blocks, pieces):
        total = sum(jnp.dot(a, w, preferred_element_type=jnp.float32) for a, w in zip(blocks, pieces))
        return total[:, step:] + swapped(total[:, :step], "c")

    outputs = []
    for pieces in chunks:
        arrived = swapped(summed(far_blocks, pieces).astype(jnp.bfloat16), "h")
        outputs.append((summed(near_blocks, pieces) + arrived.astype(jnp.float32)).astype(jnp.bfloat16))
    return jnp.concatenate(outputs, 1)


def solution(mesh):
    dp, tensor = mesh.shape["dp"], mesh.shape["tensor"]
    fine = Mesh(mesh.devices.reshape(2, dp // 8, 2, 2, 2, tensor // 2), NODE_AXES + HEAD_AXES)
    return jax.shard_map(
        per_device,
        mesh=fine,
        in_specs=(
            P(NODE_AXES, HEAD_AXES),
            P(None, NODE_AXES, HEAD_AXES),
            P(HEAD_AXES + NODE_AXES, None),
            P(),
            P(),
        ),
        out_specs=P(NODE_AXES, HEAD_AXES),
        check_vma=False,
    )
```

```python
import functools

import jax
import jax.numpy as jnp
from jax import lax
from jax.experimental import pallas as pl
from jax.experimental.pallas import tpu as pltpu
from jax.sharding import Mesh
from jax.sharding import PartitionSpec as P

HEAD_DIM = 128
ANC = 3
NEG_BIG = -1e30
CHUNKS = 2

NODE_AXES = ("h", "q", "l", "x")
HEAD_AXES = ("y", "c")


def swapped(value, axis):
    return lax.ppermute(value, axis, [(0, 1), (1, 0)])


def passed_along(value, by):
    size = lax.axis_size(NODE_AXES)
    return lax.ppermute(value, NODE_AXES, [(i, (i + by) % size) for i in range(size)])


def attend_kernel(where_ref, parents_ref, lengths_ref, query_ref, *refs):
    kv_refs, out_ref = refs[: ANC + 1], refs[ANC + 1]
    node = where_ref[1]
    capacity = query_ref.shape[0]
    kv_count = kv_refs[0].shape[2] // HEAD_DIM
    per_group = query_ref.shape[1] // HEAD_DIM // kv_count
    score_scale = HEAD_DIM ** (-0.5)
    limits = [lengths_ref[node]] + [jnp.int32(0)] * ANC
    climber = parents_ref[node]
    for _ in range(ANC):
        reached = jnp.maximum(climber, 0)
        for distance in range(1, ANC + 1):
            hit = (climber >= 0) & (node - climber == distance)
            limits[distance] = jnp.where(hit, lengths_ref[reached], limits[distance])
        climber = jnp.where(climber >= 0, parents_ref[reached], -1)
    row = lax.broadcasted_iota(jnp.int32, (capacity, capacity), 0)
    col = lax.broadcasted_iota(jnp.int32, (capacity, capacity), 1)
    masks = [(col <= row) & (col < limits[0])] + [col < limits[d] for d in range(1, ANC + 1)]
    live = lax.broadcasted_iota(jnp.int32, (capacity, HEAD_DIM), 0) < limits[0]
    for kv_head in range(kv_count):
        kv_cols = slice(kv_head * HEAD_DIM, (kv_head + 1) * HEAD_DIM)
        for member in range(per_group):
            head = kv_head * per_group + member
            cols = slice(head * HEAD_DIM, (head + 1) * HEAD_DIM)
            q = query_ref[:, cols]
            scores = []
            for kv_ref, mask in zip(kv_refs, masks):
                s = lax.dot_general(
                    q, kv_ref[0, :, kv_cols], (((1,), (1,)), ((), ())), preferred_element_type=jnp.float32
                )
                scores.append(jnp.where(mask, s * score_scale, NEG_BIG))
            row_max = functools.reduce(jnp.maximum, scores).max(axis=1, keepdims=True)
            weights = [jnp.exp(s - row_max) for s in scores]
            row_sum = functools.reduce(jnp.add, weights).sum(axis=1, keepdims=True)
            total = jnp.zeros((capacity, HEAD_DIM), jnp.float32)
            for kv_ref, w in zip(kv_refs, weights):
                total = total + jnp.dot(
                    w.astype(jnp.bfloat16), kv_ref[1, :, kv_cols], preferred_element_type=jnp.float32
                )
            out_ref[:, cols] = jnp.where(live, total / row_sum, 0.0).astype(out_ref.dtype)


def attend(half, node, parents, lengths, query, kv_blocks):
    capacity, width = query.shape[0], query.shape[1] // 2
    kv_width = kv_blocks[0].shape[2] // 2
    return pl.pallas_call(
        attend_kernel,
        out_shape=jax.ShapeDtypeStruct((capacity, width), jnp.bfloat16),
        grid_spec=pltpu.PrefetchScalarGridSpec(
            num_scalar_prefetch=3,
            grid=(1,),
            in_specs=[pl.BlockSpec((capacity, width), lambda i, w, p, n: (0, w[0]))]
            + [pl.BlockSpec((2, capacity, kv_width), lambda i, w, p, n: (0, 0, w[0]))] * (ANC + 1),
            out_specs=pl.BlockSpec((capacity, width), lambda i, w, p, n: (0, 0)),
        ),
        compiler_params=pltpu.CompilerParams(vmem_limit_bytes=8 * 2**20),
        cost_estimate=pl.CostEstimate(
            flops=capacity * capacity * (ANC + 1) * width,
            bytes_accessed=4 * capacity * width + 4 * capacity * kv_width * (ANC + 1),
            transcendentals=capacity * capacity * (ANC + 1) * width // HEAD_DIM,
        ),
    )(jnp.stack([half, node]).astype(jnp.int32), parents, lengths, query, *kv_blocks)


def project_kernel(where_ref, far_ref, far_y_ref, near_ref, near_y_ref, *refs):
    pieces, (theirs_ref, mine_ref, weight_ref) = refs[:8], refs[8:]
    rows, depth = pieces[0].shape[0], far_ref.shape[1]
    tokens, half = far_ref.shape[0], theirs_ref.shape[1]
    for i, piece in enumerate(pieces):
        block = where_ref[0] ^ (i % 4)
        start = pl.multiple_of(block * rows + (i // 4) * depth, 32)
        weight_ref[pl.ds(start, rows), :] = piece[...]
    for place, (a_ref, b_ref) in enumerate([(far_ref, far_y_ref), (near_ref, near_y_ref)]):
        out_rows = slice(place * tokens, (place + 1) * tokens)
        for out_ref, cols in ((theirs_ref, slice(0, half)), (mine_ref, slice(half, 2 * half))):
            total = jnp.dot(a_ref[...], weight_ref[:depth, cols], preferred_element_type=jnp.float32)
            total = total + jnp.dot(b_ref[...], weight_ref[depth:, cols], preferred_element_type=jnp.float32)
            out_ref[out_rows, :] = total


def project(place, inputs, pieces):
    tokens, depth = inputs[0].shape
    columns = pieces[0].shape[1]
    vmem = pl.BlockSpec(memory_space=pltpu.VMEM)
    out = jax.ShapeDtypeStruct((2 * tokens, columns // 2), jnp.float32)
    return pl.pallas_call(
        project_kernel,
        out_shape=(out, out),
        in_specs=[pl.BlockSpec(memory_space=pltpu.SMEM)] + [vmem] * (len(inputs) + len(pieces)),
        out_specs=(vmem, vmem),
        scratch_shapes=[pltpu.VMEM((2 * depth, columns), jnp.bfloat16)],
        compiler_params=pltpu.CompilerParams(vmem_limit_bytes=24 * 2**20),
        cost_estimate=pl.CostEstimate(
            flops=2 * tokens * 2 * depth * columns,
            bytes_accessed=4 * depth * columns + 8 * tokens * columns,
            transcendentals=0,
        ),
    )(jnp.reshape(place, (1,)).astype(jnp.int32), *inputs, *pieces)


def per_device(query, keys_values, out_weight, parents, lengths):
    h, l, x = lax.axis_index("h"), lax.axis_index("l"), lax.axis_index("x")
    y, c = lax.axis_index("y"), lax.axis_index("c")
    node = lax.axis_index(NODE_AXES)
    kv_blocks = [keys_values] + [passed_along(keys_values, d) for d in range(1, ANC + 1)]

    parts = lax.axis_size("q")
    if parts > 1:
        out_weight = lax.all_gather(out_weight, "q", axis=0, tiled=True)
    width = out_weight.shape[1] // 4
    step = width // CHUNKS

    def chunk_of(y_index, chunk):
        starts = [(y_index * 2 + c_index) * width + chunk * step for c_index in (1 - c, c)]
        return jnp.concatenate([lax.dynamic_slice_in_dim(out_weight, s, step, 1) for s in starts], 1)

    chunks = []
    for chunk in range(CHUNKS):
        own_y = swapped(chunk_of(1 - y, chunk), "y")
        own = chunk_of(y, chunk)
        own_x, own_l = swapped(own, "x"), swapped(own, "l")
        y_x, y_l = swapped(own_y, "x"), swapped(own_y, "l")
        own_lx, y_lx = swapped(own_l, "x"), swapped(y_x, "l")
        chunks.append([own, own_x, own_l, own_lx, own_y, y_x, y_l, y_lx])

    sent = attend(1 - h, node, parents, lengths, query, kv_blocks)
    far = swapped(sent, "h")
    near = attend(h, node, parents, lengths, query, kv_blocks)

    def ordered(attended):
        if parts == 1:
            return attended
        split = attended.reshape(attended.shape[0], parts, 4, -1)
        return jnp.swapaxes(split, 1, 2).reshape(attended.shape)

    near, far = ordered(near), ordered(far)
    tokens = near.shape[0]
    inputs = [far, swapped(far, "y"), near, swapped(near, "y")]
    outputs = []
    for pieces in chunks:
        theirs, mine = project(l * 2 + x, inputs, pieces)
        both = mine + swapped(theirs, "c")
        arrived = swapped(both[:tokens].astype(jnp.bfloat16), "h")
        outputs.append((both[tokens:] + arrived.astype(jnp.float32)).astype(jnp.bfloat16))
    return jnp.concatenate(outputs, 1)


def solution(mesh):
    dp, tensor = mesh.shape["dp"], mesh.shape["tensor"]
    fine = Mesh(mesh.devices.reshape(2, dp // 8, 2, 2, 2, tensor // 2), NODE_AXES + HEAD_AXES)
    return jax.shard_map(
        per_device,
        mesh=fine,
        in_specs=(
            P(NODE_AXES, HEAD_AXES),
            P(None, NODE_AXES, HEAD_AXES),
            P(HEAD_AXES + NODE_AXES, None),
            P(),
            P(),
        ),
        out_specs=P(NODE_AXES, HEAD_AXES),
        check_vma=False,
    )
```

```python
import functools

import jax
import jax.numpy as jnp
from jax import lax
from jax.experimental import pallas as pl
from jax.experimental.pallas import tpu as pltpu
from jax.sharding import Mesh
from jax.sharding import PartitionSpec as P

HEAD_DIM = 128
ANC = 3
NEG_BIG = -1e30
CHUNKS = (0,5,10)

NODE_AXES = ("h", "q", "l", "x")
HEAD_AXES = ("y", "c")


def swapped(value, axis):
    return lax.ppermute(value, axis, [(0, 1), (1, 0)])


def passed_along(value, by):
    size = lax.axis_size(NODE_AXES)
    return lax.ppermute(value, NODE_AXES, [(i, (i + by) % size) for i in range(size)])


def attend_kernel(where_ref, parents_ref, lengths_ref, query_ref, *refs):
    kv_refs, out_ref = refs[: ANC + 1], refs[ANC + 1]
    node = where_ref[1]
    capacity = query_ref.shape[0]
    kv_count = kv_refs[0].shape[2] // HEAD_DIM
    per_group = query_ref.shape[1] // HEAD_DIM // kv_count
    score_scale = HEAD_DIM ** (-0.5)
    limits = [lengths_ref[node]] + [jnp.int32(0)] * ANC
    climber = parents_ref[node]
    for _ in range(ANC):
        reached = jnp.maximum(climber, 0)
        for distance in range(1, ANC + 1):
            hit = (climber >= 0) & (node - climber == distance)
            limits[distance] = jnp.where(hit, lengths_ref[reached], limits[distance])
        climber = jnp.where(climber >= 0, parents_ref[reached], -1)
    row = lax.broadcasted_iota(jnp.int32, (capacity, capacity), 0)
    col = lax.broadcasted_iota(jnp.int32, (capacity, capacity), 1)
    masks = [(col <= row) & (col < limits[0])] + [col < limits[d] for d in range(1, ANC + 1)]
    live = lax.broadcasted_iota(jnp.int32, (capacity, HEAD_DIM), 0) < limits[0]
    for kv_head in range(kv_count):
        kv_cols = slice(kv_head * HEAD_DIM, (kv_head + 1) * HEAD_DIM)
        for member in range(per_group):
            head = kv_head * per_group + member
            cols = slice(head * HEAD_DIM, (head + 1) * HEAD_DIM)
            q = query_ref[:, cols]
            scores = []
            for kv_ref, mask in zip(kv_refs, masks):
                s = lax.dot_general(
                    q, kv_ref[0, :, kv_cols], (((1,), (1,)), ((), ())), preferred_element_type=jnp.float32
                )
                scores.append(jnp.where(mask, s * score_scale, NEG_BIG))
            row_max = functools.reduce(jnp.maximum, scores).max(axis=1, keepdims=True)
            weights = [jnp.exp(s - row_max) for s in scores]
            row_sum = functools.reduce(jnp.add, weights).sum(axis=1, keepdims=True)
            total = jnp.zeros((capacity, HEAD_DIM), jnp.float32)
            for kv_ref, w in zip(kv_refs, weights):
                total = total + jnp.dot(
                    w.astype(jnp.bfloat16), kv_ref[1, :, kv_cols], preferred_element_type=jnp.float32
                )
            out_ref[:, cols] = jnp.where(live, total / row_sum, 0.0).astype(out_ref.dtype)


def attend(half, node, parents, lengths, query, kv_blocks):
    capacity, width = query.shape[0], query.shape[1] // 2
    kv_width = kv_blocks[0].shape[2] // 2
    return pl.pallas_call(
        attend_kernel,
        out_shape=jax.ShapeDtypeStruct((capacity, width), jnp.bfloat16),
        grid_spec=pltpu.PrefetchScalarGridSpec(
            num_scalar_prefetch=3,
            grid=(1,),
            in_specs=[pl.BlockSpec((capacity, width), lambda i, w, p, n: (0, w[0]))]
            + [pl.BlockSpec((2, capacity, kv_width), lambda i, w, p, n: (0, 0, w[0]))] * (ANC + 1),
            out_specs=pl.BlockSpec((capacity, width), lambda i, w, p, n: (0, 0)),
        ),
        compiler_params=pltpu.CompilerParams(vmem_limit_bytes=8 * 2**20),
        cost_estimate=pl.CostEstimate(
            flops=0,
            bytes_accessed=0,
            transcendentals=0,
        ),
    )(jnp.stack([half, node]).astype(jnp.int32), parents, lengths, query, *kv_blocks)


def project_kernel(where_ref, far_ref, far_y_ref, near_ref, near_y_ref, *refs):
    pieces, (far_theirs_ref, far_mine_ref, near_theirs_ref, near_mine_ref, weight_ref) = refs[:8], refs[8:]
    rows, depth = pieces[0].shape[0], far_ref.shape[1]
    half = far_mine_ref.shape[1]
    for i, piece in enumerate(pieces):
        block = where_ref[0] ^ (i % 4)
        start = pl.multiple_of(block * rows + (i // 4) * depth, 32)
        weight_ref[pl.ds(start, rows), :] = piece[...]
    for a_ref, b_ref, theirs_ref, mine_ref in (
        (far_ref, far_y_ref, far_theirs_ref, far_mine_ref),
        (near_ref, near_y_ref, near_theirs_ref, near_mine_ref),
    ):
        for out_ref, cols in ((theirs_ref, slice(0, half)), (mine_ref, slice(half, 2 * half))):
            total = jnp.dot(a_ref[...], weight_ref[:depth, cols], preferred_element_type=jnp.float32)
            total = total + jnp.dot(b_ref[...], weight_ref[depth:, cols], preferred_element_type=jnp.float32)
            out_ref[...] = total.astype(out_ref.dtype)


def project(place, inputs, pieces):
    tokens, depth = inputs[0].shape
    columns = pieces[0].shape[1]
    vmem = pl.BlockSpec(memory_space=pltpu.VMEM)
    out = jax.ShapeDtypeStruct((tokens, columns // 2), jnp.float32)
    sent = jax.ShapeDtypeStruct((tokens, columns // 2), jnp.float32)
    return pl.pallas_call(
        project_kernel,
        out_shape=(sent, out, sent, out),
        in_specs=[pl.BlockSpec(memory_space=pltpu.SMEM)] + [vmem] * (len(inputs) + len(pieces)),
        out_specs=(vmem,) * 4,
        scratch_shapes=[pltpu.VMEM((2 * depth, columns), jnp.bfloat16)],
        compiler_params=pltpu.CompilerParams(vmem_limit_bytes=24 * 2**20),
        cost_estimate=pl.CostEstimate(
            flops=0,
            bytes_accessed=0,
            transcendentals=0,
        ),
    )(jnp.reshape(place, (1,)).astype(jnp.int32), *inputs, *pieces)


def per_device(query, keys_values, out_weight, parents, lengths):
    h, l, x = lax.axis_index("h"), lax.axis_index("l"), lax.axis_index("x")
    y, c = lax.axis_index("y"), lax.axis_index("c")
    node = lax.axis_index(NODE_AXES)
    kv_blocks = [keys_values] + [passed_along(keys_values, d) for d in range(1, ANC + 1)]

    parts = lax.axis_size("q")
    if parts > 1:
        out_weight = lax.all_gather(out_weight, "q", axis=0, tiled=True)
    width = out_weight.shape[1] // 4
    bounds = [width // CHUNKS[-1] * place for place in CHUNKS]

    def chunk_of(y_index, begin, end):
        starts = [(y_index * 2 + c_index) * width + begin for c_index in (1 - c, c)]
        return jnp.concatenate([lax.dynamic_slice_in_dim(out_weight, s, end - begin, 1) for s in starts], 1)

    chunks = []
    for chunk in zip(bounds[:-1], bounds[1:]):
        own_y = swapped(chunk_of(1 - y, *chunk), "y")
        own = chunk_of(y, *chunk)
        own_x, own_l = swapped(own, "x"), swapped(own, "l")
        y_x, y_l = swapped(own_y, "x"), swapped(own_y, "l")
        own_lx, y_lx = swapped(own_l, "x"), swapped(y_x, "l")
        chunks.append([own, own_x, own_l, own_lx, own_y, y_x, y_l, y_lx])

    def after(value, pins):
        value, picked = lax.optimization_barrier((value, [chunks[j][i] for j, i in pins]))
        for (j, i), piece in zip(pins, picked):
            chunks[j][i] = piece
        return value

    sent = attend(1 - h, node, parents, lengths, query, kv_blocks)
    far = swapped(sent, "h")
    near = attend(h, node, parents, lengths, query, kv_blocks)

    def ordered(attended):
        if parts == 1:
            return attended
        split = attended.reshape(attended.shape[0], parts, 4, -1)
        return jnp.swapaxes(split, 1, 2).reshape(attended.shape)

    near, far = ordered(near), ordered(far)
    inputs = [far, swapped(far, "y"), near, swapped(near, "y")]
    outputs = []
    for number, pieces in enumerate(chunks):
        far_theirs, far_mine, near_theirs, near_mine = project(l * 2 + x, inputs, pieces)
        if number + 1 < len(chunks):
            far_sum = far_theirs + swapped(far_mine.astype(jnp.bfloat16), "c").astype(jnp.float32)
            arrived = swapped(far_sum.astype(jnp.bfloat16), "h")
            total = near_mine + swapped(near_theirs + arrived.astype(jnp.float32), "c")
        else:
            far_sum = far_mine + swapped(far_theirs.astype(jnp.bfloat16), "c").astype(jnp.float32)
            near_sum = near_mine + swapped(near_theirs, "c")
            arrived = swapped(far_sum.astype(jnp.bfloat16), "h")
            total = near_sum + arrived.astype(jnp.float32)
        outputs.append(total.astype(jnp.bfloat16))
    return jnp.concatenate(outputs, 1)


def solution(mesh):
    dp, tensor = mesh.shape["dp"], mesh.shape["tensor"]
    fine = Mesh(mesh.devices.reshape(2, dp // 8, 2, 2, 2, tensor // 2), NODE_AXES + HEAD_AXES)
    return jax.shard_map(
        per_device,
        mesh=fine,
        in_specs=(
            P(NODE_AXES, HEAD_AXES),
            P(None, NODE_AXES, HEAD_AXES),
            P(HEAD_AXES + NODE_AXES, None),
            P(),
            P(),
        ),
        out_specs=P(NODE_AXES, HEAD_AXES),
        check_vma=False,
    )
```

```python
import functools

import jax
import jax.numpy as jnp
from jax import lax
from jax.experimental import pallas as pl
from jax.experimental.pallas import tpu as pltpu
from jax.sharding import Mesh
from jax.sharding import PartitionSpec as P

HEAD_DIM = 128
ANC = 3
NEG_BIG = -1e30
CHUNKS = (0,5,10)

NODE_AXES = ("h", "q", "l", "x")
HEAD_AXES = ("y", "c")


def swapped(value, axis):
    return lax.ppermute(value, axis, [(0, 1), (1, 0)])


def passed_along(value, by):
    size = lax.axis_size(NODE_AXES)
    return lax.ppermute(value, NODE_AXES, [(i, (i + by) % size) for i in range(size)])


def attend_kernel(where_ref, parents_ref, lengths_ref, query_ref, *refs):
    kv_refs, out_ref = refs[: ANC + 1], refs[ANC + 1]
    node = where_ref[1]
    capacity = query_ref.shape[0]
    kv_count = kv_refs[0].shape[2] // HEAD_DIM
    per_group = query_ref.shape[1] // HEAD_DIM // kv_count
    score_scale = HEAD_DIM ** (-0.5)
    limits = [lengths_ref[node]] + [jnp.int32(0)] * ANC
    climber = parents_ref[node]
    for _ in range(ANC):
        reached = jnp.maximum(climber, 0)
        for distance in range(1, ANC + 1):
            hit = (climber >= 0) & (node - climber == distance)
            limits[distance] = jnp.where(hit, lengths_ref[reached], limits[distance])
        climber = jnp.where(climber >= 0, parents_ref[reached], -1)
    row = lax.broadcasted_iota(jnp.int32, (capacity, capacity), 0)
    col = lax.broadcasted_iota(jnp.int32, (capacity, capacity), 1)
    masks = [(col <= row) & (col < limits[0])] + [col < limits[d] for d in range(1, ANC + 1)]
    live = lax.broadcasted_iota(jnp.int32, (capacity, HEAD_DIM), 0) < limits[0]
    for kv_head in range(kv_count):
        kv_cols = slice(kv_head * HEAD_DIM, (kv_head + 1) * HEAD_DIM)
        for member in range(per_group):
            head = kv_head * per_group + member
            cols = slice(head * HEAD_DIM, (head + 1) * HEAD_DIM)
            q = query_ref[:, cols]
            scores = []
            for kv_ref, mask in zip(kv_refs, masks):
                s = lax.dot_general(
                    q, kv_ref[0, :, kv_cols], (((1,), (1,)), ((), ())), preferred_element_type=jnp.float32
                )
                scores.append(jnp.where(mask, s * score_scale, NEG_BIG))
            row_max = functools.reduce(jnp.maximum, scores).max(axis=1, keepdims=True)
            weights = [jnp.exp(s - row_max) for s in scores]
            row_sum = functools.reduce(jnp.add, weights).sum(axis=1, keepdims=True)
            total = jnp.zeros((capacity, HEAD_DIM), jnp.float32)
            for kv_ref, w in zip(kv_refs, weights):
                total = total + jnp.dot(
                    w.astype(jnp.bfloat16), kv_ref[1, :, kv_cols], preferred_element_type=jnp.float32
                )
            out_ref[:, cols] = jnp.where(live, total / row_sum, 0.0).astype(out_ref.dtype)


def attend(half, node, parents, lengths, query, kv_blocks):
    capacity, width = query.shape[0], query.shape[1] // 2
    kv_width = kv_blocks[0].shape[2] // 2
    return pl.pallas_call(
        attend_kernel,
        out_shape=jax.ShapeDtypeStruct((capacity, width), jnp.bfloat16),
        grid_spec=pltpu.PrefetchScalarGridSpec(
            num_scalar_prefetch=3,
            grid=(1,),
            in_specs=[pl.BlockSpec((capacity, width), lambda i, w, p, n: (0, w[0]))]
            + [pl.BlockSpec((2, capacity, kv_width), lambda i, w, p, n: (0, 0, w[0]))] * (ANC + 1),
            out_specs=pl.BlockSpec((capacity, width), lambda i, w, p, n: (0, 0)),
        ),
        compiler_params=pltpu.CompilerParams(vmem_limit_bytes=8 * 2**20),
        cost_estimate=pl.CostEstimate(
            flops=0,
            bytes_accessed=0,
            transcendentals=0,
        ),
    )(jnp.stack([half, node]).astype(jnp.int32), parents, lengths, query, *kv_blocks)


def project_kernel(where_ref, far_ref, far_y_ref, near_ref, near_y_ref, *refs):
    pieces, (far_theirs_ref, far_mine_ref, near_theirs_ref, near_mine_ref, weight_ref) = refs[:8], refs[8:]
    rows, depth = pieces[0].shape[0], far_ref.shape[1]
    half = far_mine_ref.shape[1]
    for i, piece in enumerate(pieces):
        block = where_ref[0] ^ (i % 4)
        start = pl.multiple_of(block * rows + (i // 4) * depth, 32)
        weight_ref[pl.ds(start, rows), :] = piece[...]
    for a_ref, b_ref, theirs_ref, mine_ref in (
        (far_ref, far_y_ref, far_theirs_ref, far_mine_ref),
        (near_ref, near_y_ref, near_theirs_ref, near_mine_ref),
    ):
        for out_ref, cols in ((theirs_ref, slice(0, half)), (mine_ref, slice(half, 2 * half))):
            total = jnp.dot(a_ref[...], weight_ref[:depth, cols], preferred_element_type=jnp.float32)
            total = total + jnp.dot(b_ref[...], weight_ref[depth:, cols], preferred_element_type=jnp.float32)
            out_ref[...] = total.astype(out_ref.dtype)


def project(place, inputs, pieces):
    tokens, depth = inputs[0].shape
    columns = pieces[0].shape[1]
    vmem = pl.BlockSpec(memory_space=pltpu.VMEM)
    out = jax.ShapeDtypeStruct((tokens, columns // 2), jnp.float32)
    sent = jax.ShapeDtypeStruct((tokens, columns // 2), jnp.float32)
    return pl.pallas_call(
        project_kernel,
        out_shape=(sent, out, sent, out),
        in_specs=[pl.BlockSpec(memory_space=pltpu.SMEM)] + [vmem] * (len(inputs) + len(pieces)),
        out_specs=(vmem,) * 4,
        scratch_shapes=[pltpu.VMEM((2 * depth, columns), jnp.bfloat16)],
        compiler_params=pltpu.CompilerParams(vmem_limit_bytes=24 * 2**20),
        cost_estimate=pl.CostEstimate(
            flops=0,
            bytes_accessed=0,
            transcendentals=0,
        ),
    )(jnp.reshape(place, (1,)).astype(jnp.int32), *inputs, *pieces)


def per_device(query, keys_values, out_weight, parents, lengths):
    h, l, x = lax.axis_index("h"), lax.axis_index("l"), lax.axis_index("x")
    y, c = lax.axis_index("y"), lax.axis_index("c")
    node = lax.axis_index(NODE_AXES)
    kv_blocks = [keys_values] + [passed_along(keys_values, d) for d in range(1, ANC + 1)]

    parts = lax.axis_size("q")
    if parts > 1:
        out_weight = lax.all_gather(out_weight, "q", axis=0, tiled=True)
    width = out_weight.shape[1] // 4
    bounds = [width // CHUNKS[-1] * place for place in CHUNKS]

    def chunk_of(y_index, begin, end):
        starts = [(y_index * 2 + c_index) * width + begin for c_index in (1 - c, c)]
        return jnp.concatenate([lax.dynamic_slice_in_dim(out_weight, s, end - begin, 1) for s in starts], 1)

    chunks = []
    for chunk in zip(bounds[:-1], bounds[1:]):
        own_y = swapped(chunk_of(1 - y, *chunk), "y")
        own = chunk_of(y, *chunk)
        own_x, own_l = swapped(own, "x"), swapped(own, "l")
        y_x, y_l = swapped(own_y, "x"), swapped(own_y, "l")
        own_lx, y_lx = swapped(own_x, "l"), swapped(y_l, "x")
        chunks.append([own, own_x, own_l, own_lx, own_y, y_x, y_l, y_lx])

    def after(value, pins):
        value, picked = lax.optimization_barrier((value, [chunks[j][i] for j, i in pins]))
        for (j, i), piece in zip(pins, picked):
            chunks[j][i] = piece
        return value

    sent = attend(1 - h, node, parents, lengths, query, kv_blocks)
    far = swapped(sent, "h")
    near = attend(h, node, parents, lengths, query, kv_blocks)

    def ordered(attended):
        if parts == 1:
            return attended
        split = attended.reshape(attended.shape[0], parts, 4, -1)
        return jnp.swapaxes(split, 1, 2).reshape(attended.shape)

    near, far = ordered(near), ordered(far)
    inputs = [far, swapped(far, "y"), near, swapped(near, "y")]
    outputs = []
    for number, pieces in enumerate(chunks):
        far_theirs, far_mine, near_theirs, near_mine = project(l * 2 + x, inputs, pieces)
        if number + 1 < len(chunks):
            far_sum = far_theirs + swapped(far_mine.astype(jnp.bfloat16), "c").astype(jnp.float32)
            arrived = swapped(far_sum.astype(jnp.bfloat16), "h")
            total = near_mine + swapped(near_theirs + arrived.astype(jnp.float32), "c")
        else:
            far_sum = far_mine + swapped(far_theirs.astype(jnp.bfloat16), "c").astype(jnp.float32)
            near_sum = near_mine + swapped(near_theirs, "c")
            arrived = swapped(far_sum.astype(jnp.bfloat16), "h")
            total = near_sum + arrived.astype(jnp.float32)
        outputs.append(total.astype(jnp.bfloat16))
    return jnp.concatenate(outputs, 1)


def solution(mesh):
    dp, tensor = mesh.shape["dp"], mesh.shape["tensor"]
    fine = Mesh(mesh.devices.reshape(2, dp // 8, 2, 2, 2, tensor // 2), NODE_AXES + HEAD_AXES)
    return jax.shard_map(
        per_device,
        mesh=fine,
        in_specs=(
            P(NODE_AXES, HEAD_AXES),
            P(None, NODE_AXES, HEAD_AXES),
            P(HEAD_AXES + NODE_AXES, None),
            P(),
            P(),
        ),
        out_specs=P(NODE_AXES, HEAD_AXES),
        check_vma=False,
    )
```

```python
import functools

import jax
import jax.numpy as jnp
from jax import lax
from jax.experimental import pallas as pl
from jax.experimental.pallas import tpu as pltpu
from jax.sharding import Mesh
from jax.sharding import PartitionSpec as P

HEAD_DIM = 128
ANC = 3
LAST_FLOPS = 1_850_000_000
NEG_BIG = -1e30
CHUNKS = (0,5,10)

NODE_AXES = ("h", "q", "l", "x")
HEAD_AXES = ("y", "c")


def swapped(value, axis):
    return lax.ppermute(value, axis, [(0, 1), (1, 0)])


def passed_along(value, by):
    size = lax.axis_size(NODE_AXES)
    return lax.ppermute(value, NODE_AXES, [(i, (i + by) % size) for i in range(size)])


def attend_kernel(where_ref, parents_ref, lengths_ref, query_ref, *refs):
    kv_refs, out_ref = refs[: ANC + 1], refs[ANC + 1]
    node = where_ref[1]
    capacity = query_ref.shape[0]
    kv_count = kv_refs[0].shape[2] // HEAD_DIM
    per_group = query_ref.shape[1] // HEAD_DIM // kv_count
    score_scale = HEAD_DIM ** (-0.5)
    limits = [lengths_ref[node]] + [jnp.int32(0)] * ANC
    climber = parents_ref[node]
    for _ in range(ANC):
        reached = jnp.maximum(climber, 0)
        for distance in range(1, ANC + 1):
            hit = (climber >= 0) & (node - climber == distance)
            limits[distance] = jnp.where(hit, lengths_ref[reached], limits[distance])
        climber = jnp.where(climber >= 0, parents_ref[reached], -1)
    row = lax.broadcasted_iota(jnp.int32, (capacity, capacity), 0)
    col = lax.broadcasted_iota(jnp.int32, (capacity, capacity), 1)
    masks = [(col <= row) & (col < limits[0])] + [col < limits[d] for d in range(1, ANC + 1)]
    live = lax.broadcasted_iota(jnp.int32, (capacity, HEAD_DIM), 0) < limits[0]
    for kv_head in range(kv_count):
        kv_cols = slice(kv_head * HEAD_DIM, (kv_head + 1) * HEAD_DIM)
        for member in range(per_group):
            head = kv_head * per_group + member
            cols = slice(head * HEAD_DIM, (head + 1) * HEAD_DIM)
            q = query_ref[:, cols]
            scores = []
            for kv_ref, mask in zip(kv_refs, masks):
                s = lax.dot_general(
                    q, kv_ref[0, :, kv_cols], (((1,), (1,)), ((), ())), preferred_element_type=jnp.float32
                )
                scores.append(jnp.where(mask, s * score_scale, NEG_BIG))
            row_max = functools.reduce(jnp.maximum, scores).max(axis=1, keepdims=True)
            weights = [jnp.exp(s - row_max) for s in scores]
            row_sum = functools.reduce(jnp.add, weights).sum(axis=1, keepdims=True)
            total = jnp.zeros((capacity, HEAD_DIM), jnp.float32)
            for kv_ref, w in zip(kv_refs, weights):
                total = total + jnp.dot(
                    w.astype(jnp.bfloat16), kv_ref[1, :, kv_cols], preferred_element_type=jnp.float32
                )
            out_ref[:, cols] = jnp.where(live, total / row_sum, 0.0).astype(out_ref.dtype)


def attend(half, node, parents, lengths, query, kv_blocks):
    capacity, width = query.shape[0], query.shape[1] // 2
    kv_width = kv_blocks[0].shape[2] // 2
    return pl.pallas_call(
        attend_kernel,
        out_shape=jax.ShapeDtypeStruct((capacity, width), jnp.bfloat16),
        grid_spec=pltpu.PrefetchScalarGridSpec(
            num_scalar_prefetch=3,
            grid=(1,),
            in_specs=[pl.BlockSpec((capacity, width), lambda i, w, p, n: (0, w[0]))]
            + [pl.BlockSpec((2, capacity, kv_width), lambda i, w, p, n: (0, 0, w[0]))] * (ANC + 1),
            out_specs=pl.BlockSpec((capacity, width), lambda i, w, p, n: (0, 0)),
        ),
        compiler_params=pltpu.CompilerParams(vmem_limit_bytes=8 * 2**20),
        cost_estimate=pl.CostEstimate(
            flops=0,
            bytes_accessed=0,
            transcendentals=0,
        ),
    )(jnp.stack([half, node]).astype(jnp.int32), parents, lengths, query, *kv_blocks)


def project_kernel(where_ref, far_ref, far_y_ref, near_ref, near_y_ref, *refs):
    pieces, (far_theirs_ref, far_mine_ref, near_theirs_ref, near_mine_ref, weight_ref) = refs[:8], refs[8:]
    rows, depth = pieces[0].shape[0], far_ref.shape[1]
    half = far_mine_ref.shape[1]
    for i, piece in enumerate(pieces):
        block = where_ref[0] ^ (i % 4)
        start = pl.multiple_of(block * rows + (i // 4) * depth, 32)
        weight_ref[pl.ds(start, rows), :] = piece[...]
    for a_ref, b_ref, theirs_ref, mine_ref in (
        (far_ref, far_y_ref, far_theirs_ref, far_mine_ref),
        (near_ref, near_y_ref, near_theirs_ref, near_mine_ref),
    ):
        for out_ref, cols in ((theirs_ref, slice(0, half)), (mine_ref, slice(half, 2 * half))):
            total = jnp.dot(a_ref[...], weight_ref[:depth, cols], preferred_element_type=jnp.float32)
            total = total + jnp.dot(b_ref[...], weight_ref[depth:, cols], preferred_element_type=jnp.float32)
            out_ref[...] = total.astype(out_ref.dtype)


def project(place, inputs, pieces, flops):
    tokens, depth = inputs[0].shape
    columns = pieces[0].shape[1]
    vmem = pl.BlockSpec(memory_space=pltpu.VMEM)
    out = jax.ShapeDtypeStruct((tokens, columns // 2), jnp.float32)
    sent = jax.ShapeDtypeStruct((tokens, columns // 2), jnp.float32)
    return pl.pallas_call(
        project_kernel,
        out_shape=(sent, out, sent, out),
        in_specs=[pl.BlockSpec(memory_space=pltpu.SMEM)] + [vmem] * (len(inputs) + len(pieces)),
        out_specs=(vmem,) * 4,
        scratch_shapes=[pltpu.VMEM((2 * depth, columns), jnp.bfloat16)],
        compiler_params=pltpu.CompilerParams(vmem_limit_bytes=24 * 2**20),
        cost_estimate=pl.CostEstimate(
            flops=flops,
            bytes_accessed=0,
            transcendentals=0,
        ),
    )(jnp.reshape(place, (1,)).astype(jnp.int32), *inputs, *pieces)


def per_device(query, keys_values, out_weight, parents, lengths):
    h, l, x = lax.axis_index("h"), lax.axis_index("l"), lax.axis_index("x")
    y, c = lax.axis_index("y"), lax.axis_index("c")
    node = lax.axis_index(NODE_AXES)
    kv_blocks = [keys_values] + [passed_along(keys_values, d) for d in range(1, ANC + 1)]

    parts = lax.axis_size("q")
    if parts > 1:
        out_weight = lax.all_gather(out_weight, "q", axis=0, tiled=True)
    width = out_weight.shape[1] // 4
    bounds = [width // CHUNKS[-1] * place for place in CHUNKS]

    def chunk_of(y_index, begin, end):
        starts = [(y_index * 2 + c_index) * width + begin for c_index in (1 - c, c)]
        return jnp.concatenate([lax.dynamic_slice_in_dim(out_weight, s, end - begin, 1) for s in starts], 1)

    chunks = []
    for chunk in zip(bounds[:-1], bounds[1:]):
        own_y = swapped(chunk_of(1 - y, *chunk), "y")
        own = chunk_of(y, *chunk)
        own_x, own_l = swapped(own, "x"), swapped(own, "l")
        y_x, y_l = swapped(own_y, "x"), swapped(own_y, "l")
        own_lx, y_lx = swapped(own_x, "l"), swapped(y_l, "x")
        chunks.append([own, own_x, own_l, own_lx, own_y, y_x, y_l, y_lx])

    def after(value, pins):
        value, picked = lax.optimization_barrier((value, [chunks[j][i] for j, i in pins]))
        for (j, i), piece in zip(pins, picked):
            chunks[j][i] = piece
        return value

    sent = attend(1 - h, node, parents, lengths, query, kv_blocks)
    far = swapped(sent, "h")
    near = attend(h, node, parents, lengths, query, kv_blocks)

    def ordered(attended):
        if parts == 1:
            return attended
        split = attended.reshape(attended.shape[0], parts, 4, -1)
        return jnp.swapaxes(split, 1, 2).reshape(attended.shape)

    near, far = ordered(near), ordered(far)
    inputs = [far, swapped(far, "y"), near, swapped(near, "y")]
    outputs = []
    for number, pieces in enumerate(chunks):
        far_theirs, far_mine, near_theirs, near_mine = project(l * 2 + x, inputs, pieces, LAST_FLOPS if number + 1 == len(chunks) else 0)
        if number + 1 < len(chunks):
            far_sum = far_theirs + swapped(far_mine.astype(jnp.bfloat16), "c").astype(jnp.float32)
            arrived = swapped(far_sum.astype(jnp.bfloat16), "h")
            total = near_mine + swapped(near_theirs + arrived.astype(jnp.float32), "c")
        else:
            far_sum = far_mine + swapped(far_theirs.astype(jnp.bfloat16), "c").astype(jnp.float32)
            near_sum = near_mine + swapped(near_theirs, "c")
            arrived = swapped(far_sum.astype(jnp.bfloat16), "h")
            total = near_sum + arrived.astype(jnp.float32)
        outputs.append(total.astype(jnp.bfloat16))
    return jnp.concatenate(outputs, 1)


def solution(mesh):
    dp, tensor = mesh.shape["dp"], mesh.shape["tensor"]
    fine = Mesh(mesh.devices.reshape(2, dp // 8, 2, 2, 2, tensor // 2), NODE_AXES + HEAD_AXES)
    return jax.shard_map(
        per_device,
        mesh=fine,
        in_specs=(
            P(NODE_AXES, HEAD_AXES),
            P(None, NODE_AXES, HEAD_AXES),
            P(HEAD_AXES + NODE_AXES, None),
            P(),
            P(),
        ),
        out_specs=P(NODE_AXES, HEAD_AXES),
        check_vma=False,
    )
```
